32 devices in a mesh: expert: 8 (over z, y), unit: 4 (over x, core).
Axes of the slice: x: 2, y: 2, z: 4, core: 2. Of those that a mesh axis runs over, the one named last changes fastest.
Arguments:
- w_up: bfloat16 [32, 1536, 4096], P('expert', 'unit'), may hold values from -0.09375 to 0.09375
- cluster: int32 [32, 1], replicated, may hold values from 0 to 7
- counts: int32 [32], replicated, may hold values from 16 to 127
Outputs:
- merged: bfloat16 [8, 1536, 4096], P('expert', None, 'unit')
The draws below stay inside these ranges and needn't reach their ends.
Inputs may be any that keep to these rules, and one draw needn't show every extreme that they name: Every cluster has at least one member.
All inputs are finite; a program needn't handle non-finite values.
Results may differ from the reference program's by a relative error of at most 0.0051.
Values may be sent and summed in bfloat16 or wider, within the bound.
A program may use at most 128 MiB of HBM per device.

```python
import jax
import jax.numpy as jnp
from jax import lax

D = 4096
FF = 1536
BLOCK = 96
NS_STEPS = 8
EXPERTS = 32
CLUSTERS = 8


def with_ends(entries, key, least, high):
    index_at = [jax.random.randint(jax.random.fold_in(key, axis), (), 0, length) for axis, length in enumerate(entries.shape)]
    main_axis = entries.shape.index(max(entries.shape))
    beside = index_at[:main_axis] + [(index_at[main_axis] + 1) % entries.shape[main_axis]] + index_at[main_axis + 1:]
    return entries.at[tuple(index_at)].set(least).at[tuple(beside)].set(high)


def shard_levels(key, dims, split, low, largest):
    def one(position, shards_of):
        steps = jax.random.uniform(jax.random.fold_in(jax.random.fold_in(key, 6), position), (shards_of,), jnp.float32, low / len(split), largest / len(split))
        return jnp.repeat(jnp.exp(steps), dims[position] // shards_of).reshape((-1,) + (1,) * (len(dims) - position - 1))

    level = one(*split[0])
    for cut in split[1:]:
        level = level * one(*cut)
    return level


def choose_distinct(key, rows, number_of, top, lift):
    sequence = jax.random.permutation(jax.random.fold_in(key, 1), number_of)
    boost = sequence
    for power in range(3):
        boost = boost * boost // number_of
    boost = boost * lift // number_of
    tickets = jax.random.randint(jax.random.fold_in(key, 2), (rows, number_of), 0, 4096) + boost
    fixed_rows = jax.random.permutation(jax.random.fold_in(key, 3), rows)[jnp.arange(number_of) % rows]
    tickets = jnp.where(jnp.arange(rows)[:, None] == fixed_rows[None, :], 1 << 14, tickets)
    merit = tickets * number_of + jnp.arange(number_of)
    return lax.top_k(merit.astype(jnp.int32), top)[1].astype(jnp.int32)


def bell_draw(rng, dims, scale, bound, cuts=(), kind=jnp.bfloat16):
    gain = shard_levels(rng, dims, cuts, -0.22, 0.18) if cuts else 1.0
    drawn = jax.random.normal(rng, dims, jnp.float32) * scale * gain
    return jnp.minimum(jnp.maximum(drawn, -bound), bound).astype(kind)


def setup_inputs(seed: int = 0) -> dict:
    seeds = jax.random.split(jax.random.key(seed), 4)
    return {
        "w_up": bell_draw(seeds[0], (EXPERTS, FF, D), D ** -0.5, 0.09375, ((0, 8), (1, 4))),
        "cluster": choose_distinct(seeds[1], EXPERTS, CLUSTERS, 1, 2048),
        "counts": with_ends(jax.random.randint(seeds[2], (EXPERTS,), 16, 128), jax.random.fold_in(seeds[2], 1), 16, 127).astype(jnp.int32),
    }


def newton_schulz(matrices):
    frob_norm = jnp.sqrt(lax.optimization_barrier(jnp.sum(matrices * matrices, axis=(-2, -1), keepdims=True)) + 1e-06)
    value = matrices / frob_norm
    for iteration in range(NS_STEPS):
        square = jnp.einsum('...ij,...kj->...ik', value, value, precision=lax.Precision.HIGHEST)
        value = 1.5 * value - 0.5 * jnp.einsum('...ik,...kj->...ij', square, value, precision=lax.Precision.HIGHEST)
    return value

def reference(w_up, cluster, counts):
    cluster_ids = cluster[:, 0]
    experts = cluster_ids.shape[0]
    index = jnp.arange(experts, dtype=jnp.int32)
    labels = jnp.arange(CLUSTERS, dtype=jnp.int32)
    member = cluster_ids[None, :] == labels[:, None]
    score = counts * experts + (experts - 1 - index)
    best = lax.optimization_barrier(jnp.max(jnp.where(member, score[None, :], -1), axis=1))
    leader = (experts - 1 - best % experts).astype(jnp.int32)
    anchor_of = leader[cluster_ids].astype(jnp.int32)
    total = lax.optimization_barrier(jnp.sum(jnp.where(member, counts[None, :], 0), axis=1)).astype(jnp.float32)
    weight = counts.astype(jnp.float32) / total[cluster_ids]
    nblocks = FF // BLOCK

    def one_expert(carry, which):
        member_rows = w_up[which].astype(jnp.float32).reshape(nblocks, BLOCK, D)
        lead_rows = w_up[anchor_of[which]].astype(jnp.float32).reshape(nblocks, BLOCK, D)
        gram = jnp.einsum('bid,bjd->bij', lead_rows, member_rows, precision=lax.Precision.HIGHEST)
        polar = newton_schulz(gram).astype(jnp.bfloat16)
        turned = jnp.einsum('bij,bjd->bid', polar.astype(jnp.float32), member_rows, precision=lax.Precision.HIGHEST)
        aligned = (turned * weight[which]).reshape(FF, D).astype(jnp.bfloat16)
        aligned = lax.optimization_barrier(aligned)
        carry = carry.at[cluster_ids[which]].add(aligned.astype(jnp.float32))
        return (carry, None)
    merged, unused = lax.scan(one_expert, jnp.zeros((CLUSTERS, FF, D), jnp.float32), index)
    return merged.astype(jnp.bfloat16)
```

```python
import functools

import jax
import jax.numpy as jnp
from jax import lax
from jax.experimental import pallas as pl
from jax.experimental.pallas import tpu as pltpu
from jax.sharding import PartitionSpec as P

BLOCK = 96
NS_STEPS = 8
MESH = pl.DeviceIdType.MESH
VMEM_BYTES = 48 * 1024 * 1024


def newton_schulz(matrices):
    frob_norm = jnp.sqrt(jnp.sum(matrices * matrices, axis=(-2, -1), keepdims=True) + 1e-06)
    value = matrices / frob_norm
    for iteration in range(NS_STEPS):
        square = jnp.einsum("...ij,...kj->...ik", value, value, precision=lax.Precision.HIGH)
        value = 1.5 * value - 0.5 * jnp.einsum(
            "...ik,...kj->...ij", square, value, precision=lax.Precision.HIGH
        )
    return value


def deal_kernel(n, g, w_ref, slab_ref, local_sem, send_sem, recv_sem):
    me, unit = lax.axis_index("expert"), lax.axis_index("unit")
    cw = slab_ref.shape[-1]
    barrier = pltpu.get_barrier_semaphore()
    for d in range(1, n):
        pl.semaphore_signal(barrier, inc=1, device_id=(lax.rem(me + d, n), unit), device_id_type=MESH)
    pl.semaphore_wait(barrier, n - 1)

    def piece(peer):
        rows = pl.ds(pl.multiple_of((peer // g) * BLOCK, BLOCK), BLOCK)
        columns = pl.ds(pl.multiple_of(lax.rem(peer, g) * cw, cw), cw)
        return w_ref.at[:, rows, columns]

    copies = []
    for d in sorted(range(1, n), key=lambda d: abs(2 * d - n)):
        peer = lax.rem(me + d, n)
        copy = pltpu.make_async_remote_copy(
            src_ref=piece(peer),
            dst_ref=slab_ref.at[me],
            send_sem=send_sem.at[d],
            recv_sem=recv_sem.at[d],
            device_id=(peer, unit),
            device_id_type=MESH,
        )
        copy.start()
        copies.append(copy)
    own = pltpu.make_async_copy(piece(me), slab_ref.at[me], local_sem)
    own.start()
    own.wait()
    for copy in copies:
        copy.wait()


def deal(w, n, g):
    held, units, width = w.shape
    return pl.pallas_call(
        functools.partial(deal_kernel, n, g),
        out_shape=jax.ShapeDtypeStruct((n, held, BLOCK, width // g), w.dtype),
        in_specs=[pl.BlockSpec(memory_space=pl.ANY)],
        out_specs=pl.BlockSpec(memory_space=pl.ANY),
        scratch_shapes=[
            pltpu.SemaphoreType.DMA,
            pltpu.SemaphoreType.DMA((n,)),
            pltpu.SemaphoreType.DMA((n,)),
        ],
        compiler_params=pltpu.CompilerParams(
            collective_id=0, has_side_effects=True, vmem_limit_bytes=VMEM_BYTES
        ),
        cost_estimate=pl.CostEstimate(flops=0, bytes_accessed=4 * w.size, transcendentals=0),
        name="deal",
    )(w)


def gram_kernel(order_ref, anchor_ref, lead_ref, rows_ref, gram_ref):
    gram_ref[0] = lax.dot_general(
        lead_ref[0], rows_ref[0], (((1,), (1,)), ((), ())), preferred_element_type=jnp.float32
    )


def block_gram(order, anchor_of, slab):
    experts, _, cw = slab.shape
    return pl.pallas_call(
        gram_kernel,
        grid_spec=pltpu.PrefetchScalarGridSpec(
            num_scalar_prefetch=2,
            grid=(experts,),
            in_specs=[
                pl.BlockSpec((1, BLOCK, cw), lambda s, order, anchor: (anchor[order[s]], 0, 0)),
                pl.BlockSpec((1, BLOCK, cw), lambda s, order, anchor: (order[s], 0, 0)),
            ],
            out_specs=pl.BlockSpec((1, BLOCK, BLOCK), lambda s, order, anchor: (order[s], 0, 0)),
        ),
        out_shape=jax.ShapeDtypeStruct((experts, BLOCK, BLOCK), jnp.float32),
        compiler_params=pltpu.CompilerParams(vmem_limit_bytes=VMEM_BYTES),
        cost_estimate=pl.CostEstimate(
            flops=2 * slab.size * BLOCK, bytes_accessed=4 * slab.size, transcendentals=0
        ),
        name="gram",
    )(order, anchor_of, slab, slab)


def merge_kernel(order_ref, cluster_ref, weight_ref, factor_ref, rows_ref, merged_ref, total_ref):
    step = pl.program_id(0)
    expert = order_ref[step]
    last = order_ref[jnp.maximum(step - 1, 0)]
    opens = (step == 0) | (cluster_ref[last] != cluster_ref[expert])
    turned = jnp.dot(factor_ref[0], rows_ref[0], preferred_element_type=jnp.float32)
    aligned = (turned * weight_ref[expert]).astype(jnp.bfloat16).astype(jnp.float32)

    @pl.when(opens)
    def _():
        total_ref[...] = aligned

    @pl.when(jnp.logical_not(opens))
    def _():
        total_ref[...] += aligned

    merged_ref[0] = total_ref[...].astype(merged_ref.dtype)


def merge_rows(order, cluster_ids, weight, factors, slab, clusters):
    experts, _, cw = slab.shape
    return pl.pallas_call(
        merge_kernel,
        grid_spec=pltpu.PrefetchScalarGridSpec(
            num_scalar_prefetch=3,
            grid=(experts,),
            in_specs=[
                pl.BlockSpec((1, BLOCK, BLOCK), lambda s, order, ids, weight: (order[s], 0, 0)),
                pl.BlockSpec((1, BLOCK, cw), lambda s, order, ids, weight: (order[s], 0, 0)),
            ],
            out_specs=pl.BlockSpec((1, BLOCK, cw), lambda s, order, ids, weight: (ids[order[s]], 0, 0)),
            scratch_shapes=[pltpu.VMEM((BLOCK, cw), jnp.float32)],
        ),
        out_shape=jax.ShapeDtypeStruct((clusters, BLOCK, cw), slab.dtype),
        compiler_params=pltpu.CompilerParams(vmem_limit_bytes=VMEM_BYTES),
        cost_estimate=pl.CostEstimate(
            flops=2 * slab.size * BLOCK, bytes_accessed=3 * slab.size, transcendentals=0
        ),
        name="merge",
    )(order, cluster_ids, weight, factors, slab)


def serve_kernel(n, m, g, units, merged_ref, out_ref, local_sem, send_sem, recv_sem):
    me, unit = lax.axis_index("expert"), lax.axis_index("unit")
    cw, uw = merged_ref.shape[-1], out_ref.shape[-1]
    pw = min(cw, uw)
    parts = cw // pw

    def target(part):
        column = lax.rem(me, g) * cw + part * pw
        return column // uw, pl.multiple_of(lax.rem(column, uw), pw)

    def feeds(source):
        column = lax.rem(source, g) * cw
        return (column // uw <= unit) & (unit <= (column + cw - pw) // uw)

    barrier = pltpu.get_barrier_semaphore()
    for d in range(n):
        source = lax.rem(me + n - d, n)
        for u in range(m):
            @pl.when(feeds(source) & ((u != unit) | (d != 0)))
            def _():
                pl.semaphore_signal(barrier, inc=1, device_id=(source, u), device_id_type=MESH)
    own = feeds(me)
    pl.semaphore_wait(barrier, n * parts - own.astype(jnp.int32))

    rows = pl.ds(pl.multiple_of(unit * units + (me // g) * BLOCK, BLOCK), BLOCK)

    def remote(d, part):
        peer = lax.rem(me + d, n)
        to, offset = target(part)
        return pltpu.make_async_remote_copy(
            src_ref=merged_ref.at[peer, :, pl.ds(part * pw, pw)],
            dst_ref=out_ref.at[0, rows, pl.ds(offset, pw)],
            send_sem=send_sem.at[d, part],
            recv_sem=recv_sem.at[d, unit],
            device_id=(peer, to),
            device_id_type=MESH,
        )

    def local(part):
        _, offset = target(part)
        return pltpu.make_async_copy(
            merged_ref.at[me, :, pl.ds(part * pw, pw)], out_ref.at[0, rows, pl.ds(offset, pw)], local_sem
        )

    for d in sorted(range(n), key=lambda d: abs(2 * d - n)):
        for part in range(parts):
            if d:
                remote(d, part).start()
            else:
                mine = target(part)[0] == unit

                @pl.when(mine)
                def _():
                    local(part).start()

                @pl.when(jnp.logical_not(mine))
                def _():
                    remote(0, part).start()

    for d in range(n):
        for part in range(parts):
            if d:
                remote(d, part).wait_send()
            else:
                mine = target(part)[0] == unit

                @pl.when(mine)
                def _():
                    local(part).wait()

                @pl.when(jnp.logical_not(mine))
                def _():
                    remote(0, part).wait_send()

    for d in range(n):
        source = lax.rem(me + n - d, n)
        for u in range(m):
            @pl.when(feeds(source) & ((u != unit) | (d != 0)))
            def _():
                there = pl.ds(pl.multiple_of(u * units + (source // g) * BLOCK, BLOCK), BLOCK)
                column = pl.multiple_of(lax.rem(lax.rem(source, g) * cw, uw), pw)
                landed = out_ref.at[0, there, pl.ds(column, pw)]
                pltpu.make_async_remote_copy(
                    src_ref=landed,
                    dst_ref=landed,
                    send_sem=send_sem.at[0, 0],
                    recv_sem=recv_sem.at[d, u],
                    device_id=(source, u),
                    device_id_type=MESH,
                ).wait_recv()


def serve(merged, n, m, g, units, width):
    parts = max(1, merged.shape[-1] * m // width)
    return pl.pallas_call(
        functools.partial(serve_kernel, n, m, g, units),
        out_shape=jax.ShapeDtypeStruct((1, m * units, width // m), merged.dtype),
        in_specs=[pl.BlockSpec(memory_space=pl.ANY)],
        out_specs=pl.BlockSpec(memory_space=pl.ANY),
        scratch_shapes=[
            pltpu.SemaphoreType.DMA,
            pltpu.SemaphoreType.DMA((n, parts)),
            pltpu.SemaphoreType.DMA((n, m)),
        ],
        compiler_params=pltpu.CompilerParams(
            collective_id=1, has_side_effects=True, vmem_limit_bytes=VMEM_BYTES
        ),
        cost_estimate=pl.CostEstimate(flops=0, bytes_accessed=4 * merged.size, transcendentals=0),
        name="serve",
    )(merged)


def on_device(w_up, cluster, counts):
    n, m = lax.axis_size("expert"), lax.axis_size("unit")
    held, units, width = w_up.shape
    nblocks = units // BLOCK
    g = n // nblocks
    cluster_ids = cluster[:, 0]
    experts = cluster_ids.shape[0]
    index = jnp.arange(experts, dtype=jnp.int32)
    labels = jnp.arange(n, dtype=jnp.int32)
    member = cluster_ids[None, :] == labels[:, None]
    score = counts * experts + (experts - 1 - index)
    best = jnp.max(jnp.where(member, score[None, :], -1), axis=1)
    leader = experts - 1 - best % experts
    anchor_of = jnp.sum(jnp.where(member, leader[:, None], 0), axis=0)
    total = jnp.sum(jnp.where(member, counts[None, :], 0), axis=1).astype(jnp.float32)
    weight = counts.astype(jnp.float32) / jnp.sum(jnp.where(member, total[:, None], 0.0), axis=0)

    slab = deal(w_up, n, g).reshape(experts, BLOCK, width // g)
    before = (cluster_ids[None, :] < cluster_ids[:, None]) | (
        (cluster_ids[None, :] == cluster_ids[:, None]) & (index[None, :] < index[:, None])
    )
    place = jnp.sum(before.astype(jnp.int32), axis=1)
    order = jnp.sum(jnp.where(place[None, :] == index[:, None], index[None, :], 0), axis=1)
    partial = block_gram(order, anchor_of, slab)

    share = experts // g
    part = lax.axis_index("expert") % g

    def pairs(d):
        return [(e, e // g * g + (e + d) % g) for e in range(n)]

    gram = lax.dynamic_slice_in_dim(partial, part * share, share)
    for d in range(1, g):
        other = lax.dynamic_slice_in_dim(partial, (part + d) % g * share, share)
        gram = gram + lax.ppermute(other, "expert", pairs(d))
    polar = newton_schulz(gram).astype(jnp.bfloat16)
    factors = jnp.zeros((experts, BLOCK, BLOCK), jnp.bfloat16)
    factors = lax.dynamic_update_slice_in_dim(factors, polar, part * share, 0)
    for d in range(1, g):
        other = lax.ppermute(polar, "expert", pairs(d))
        factors = lax.dynamic_update_slice_in_dim(factors, other, (part + g - d) % g * share, 0)

    merged = merge_rows(order, cluster_ids, weight, factors, slab, n)
    return serve(merged, n, m, g, units, width)


def solution(mesh):
    return jax.shard_map(
        on_device,
        mesh=mesh,
        in_specs=(P("expert", "unit", None), P(), P()),
        out_specs=P("expert", None, "unit"),
        check_vma=False,
    )
```

```python
import functools

import jax
import jax.numpy as jnp
from jax import lax
from jax.experimental import pallas as pl
from jax.experimental.pallas import tpu as pltpu
from jax.sharding import PartitionSpec as P

BLOCK = 96
NS_STEPS = 8
MESH = pl.DeviceIdType.MESH
VMEM_BYTES = 48 * 1024 * 1024


def newton_schulz(matrices):
    frob_norm = jnp.sqrt(jnp.sum(matrices * matrices, axis=(-2, -1), keepdims=True) + 1e-06)
    value = matrices / frob_norm
    for iteration in range(NS_STEPS):
        square = jnp.einsum("...ij,...kj->...ik", value, value, precision=lax.Precision.HIGH)
        value = 1.5 * value - 0.5 * jnp.einsum(
            "...ik,...kj->...ij", square, value, precision=lax.Precision.HIGH
        )
    return value


def deal_kernel(n, g, w_ref, slab_ref, ready_ref, local_sem, send_sem, recv_sem):
    me, unit = lax.axis_index("expert"), lax.axis_index("unit")
    cw = slab_ref.shape[-1]
    barrier = pltpu.get_barrier_semaphore()
    for d in range(1, n):
        pl.semaphore_signal(barrier, inc=1, device_id=(lax.rem(me + d, n), unit), device_id_type=MESH)
    pl.semaphore_wait(barrier, n - 1)

    def piece(peer):
        rows = pl.ds(pl.multiple_of((peer // g) * BLOCK, BLOCK), BLOCK)
        columns = pl.ds(pl.multiple_of(lax.rem(peer, g) * cw, cw), cw)
        return w_ref.at[:, rows, columns]

    copies = []
    for d in sorted(range(1, n), key=lambda d: abs(2 * d - n)):
        peer = lax.rem(me + d, n)
        copy = pltpu.make_async_remote_copy(
            src_ref=piece(peer),
            dst_ref=slab_ref.at[me],
            send_sem=send_sem.at[d],
            recv_sem=recv_sem.at[d],
            device_id=(peer, unit),
            device_id_type=MESH,
        )
        copy.start()
        copies.append(copy)
    own = pltpu.make_async_copy(piece(me), slab_ref.at[me], local_sem)
    own.start()
    own.wait()
    for copy in copies:
        copy.wait()
    ready_ref[...] = jnp.zeros_like(ready_ref)


def deal(w, n, g):
    held, _, width = w.shape
    return pl.pallas_call(
        functools.partial(deal_kernel, n, g),
        out_shape=[
            jax.ShapeDtypeStruct((n, held, BLOCK, width // g), w.dtype),
            jax.ShapeDtypeStruct((8, 128), jnp.int32),
        ],
        in_specs=[pl.BlockSpec(memory_space=pl.ANY)],
        out_specs=[pl.BlockSpec(memory_space=pl.ANY), pl.BlockSpec(memory_space=pltpu.VMEM)],
        scratch_shapes=[
            pltpu.SemaphoreType.DMA,
            pltpu.SemaphoreType.DMA((n,)),
            pltpu.SemaphoreType.DMA((n,)),
        ],
        compiler_params=pltpu.CompilerParams(
            collective_id=0, has_side_effects=True, vmem_limit_bytes=VMEM_BYTES
        ),
        cost_estimate=pl.CostEstimate(flops=0, bytes_accessed=4 * w.size, transcendentals=0),
        name="deal",
    )(w)


def gram_kernel(order_ref, anchor_ref, lead_ref, rows_ref, gram_ref):
    gram_ref[0] = lax.dot_general(
        lead_ref[0], rows_ref[0], (((1,), (1,)), ((), ())), preferred_element_type=jnp.float32
    )


def block_gram(order, anchor_of, slab):
    experts, _, cw = slab.shape
    return pl.pallas_call(
        gram_kernel,
        grid_spec=pltpu.PrefetchScalarGridSpec(
            num_scalar_prefetch=2,
            grid=(experts,),
            in_specs=[
                pl.BlockSpec((1, BLOCK, cw), lambda s, order, anchor: (anchor[order[s]], 0, 0)),
                pl.BlockSpec((1, BLOCK, cw), lambda s, order, anchor: (order[s], 0, 0)),
            ],
            out_specs=pl.BlockSpec((1, BLOCK, BLOCK), lambda s, order, anchor: (order[s], 0, 0)),
        ),
        out_shape=jax.ShapeDtypeStruct((experts, BLOCK, BLOCK), jnp.float32),
        compiler_params=pltpu.CompilerParams(vmem_limit_bytes=VMEM_BYTES),
        cost_estimate=pl.CostEstimate(
            flops=2 * slab.size * BLOCK, bytes_accessed=4 * slab.size, transcendentals=0
        ),
        name="gram",
    )(order, anchor_of, slab, slab)


def merge_kernel(order_ref, cluster_ref, weight_ref, factor_ref, rows_ref, merged_ref, total_ref):
    step = pl.program_id(0)
    expert = order_ref[step]
    last = order_ref[jnp.maximum(step - 1, 0)]
    opens = (step == 0) | (cluster_ref[last] != cluster_ref[expert])
    turned = jnp.dot(factor_ref[0], rows_ref[0], preferred_element_type=jnp.float32)
    aligned = (turned * weight_ref[expert]).astype(jnp.bfloat16).astype(jnp.float32)

    @pl.when(opens)
    def _():
        total_ref[...] = aligned

    @pl.when(jnp.logical_not(opens))
    def _():
        total_ref[...] += aligned

    merged_ref[0] = total_ref[...].astype(merged_ref.dtype)


def merge_rows(order, cluster_ids, weight, factors, slab, clusters):
    experts, _, cw = slab.shape
    return pl.pallas_call(
        merge_kernel,
        grid_spec=pltpu.PrefetchScalarGridSpec(
            num_scalar_prefetch=3,
            grid=(experts,),
            in_specs=[
                pl.BlockSpec((1, BLOCK, BLOCK), lambda s, order, ids, weight: (order[s], 0, 0)),
                pl.BlockSpec((1, BLOCK, cw), lambda s, order, ids, weight: (order[s], 0, 0)),
            ],
            out_specs=pl.BlockSpec((1, BLOCK, cw), lambda s, order, ids, weight: (ids[order[s]], 0, 0)),
            scratch_shapes=[pltpu.VMEM((BLOCK, cw), jnp.float32)],
        ),
        out_shape=jax.ShapeDtypeStruct((clusters, BLOCK, cw), slab.dtype),
        compiler_params=pltpu.CompilerParams(vmem_limit_bytes=VMEM_BYTES),
        cost_estimate=pl.CostEstimate(
            flops=2 * slab.size * BLOCK, bytes_accessed=3 * slab.size, transcendentals=0
        ),
        name="merge",
    )(order, cluster_ids, weight, factors, slab)


def serve_kernel(n, m, g, units, merged_ref, out_ref, ready_ref, local_sem, send_sem, recv_sem):
    me, unit = lax.axis_index("expert"), lax.axis_index("unit")
    cw, uw = merged_ref.shape[-1], out_ref.shape[-1]
    pw = min(cw, uw)
    parts = cw // pw

    def target(part):
        column = lax.rem(me, g) * cw + part * pw
        return column // uw, pl.multiple_of(lax.rem(column, uw), pw)

    def feeds(source):
        column = lax.rem(source, g) * cw
        return (column // uw <= unit) & (unit <= (column + cw - pw) // uw)

    barrier = pltpu.get_barrier_semaphore()
    for d in range(n):
        source = lax.rem(me + n - d, n)
        for u in range(m):
            @pl.when(feeds(source) & ((u != unit) | (d != 0)))
            def _():
                pl.semaphore_signal(barrier, inc=1, device_id=(source, u), device_id_type=MESH)
    own = feeds(me)
    pl.semaphore_wait(barrier, n * parts - own.astype(jnp.int32))

    rows = pl.ds(pl.multiple_of(unit * units + (me // g) * BLOCK, BLOCK), BLOCK)

    def remote(d, part):
        peer = lax.rem(me + d, n)
        to, offset = target(part)
        return pltpu.make_async_remote_copy(
            src_ref=merged_ref.at[peer, :, pl.ds(part * pw, pw)],
            dst_ref=out_ref.at[0, rows, pl.ds(offset, pw)],
            send_sem=send_sem.at[d, part],
            recv_sem=recv_sem.at[d, unit],
            device_id=(peer, to),
            device_id_type=MESH,
        )

    def local(part):
        _, offset = target(part)
        return pltpu.make_async_copy(
            merged_ref.at[me, :, pl.ds(part * pw, pw)], out_ref.at[0, rows, pl.ds(offset, pw)], local_sem
        )

    for d in sorted(range(n), key=lambda d: abs(2 * d - n)):
        for part in range(parts):
            if d:
                remote(d, part).start()
            else:
                mine = target(part)[0] == unit

                @pl.when(mine)
                def _():
                    local(part).start()

                @pl.when(jnp.logical_not(mine))
                def _():
                    remote(0, part).start()

    for d in range(n):
        for part in range(parts):
            if d:
                remote(d, part).wait_send()
            else:
                mine = target(part)[0] == unit

                @pl.when(mine)
                def _():
                    local(part).wait()

                @pl.when(jnp.logical_not(mine))
                def _():
                    remote(0, part).wait_send()

    for d in range(n):
        source = lax.rem(me + n - d, n)
        for u in range(m):
            @pl.when(feeds(source) & ((u != unit) | (d != 0)))
            def _():
                there = pl.ds(pl.multiple_of(u * units + (source // g) * BLOCK, BLOCK), BLOCK)
                column = pl.multiple_of(lax.rem(lax.rem(source, g) * cw, uw), pw)
                landed = out_ref.at[0, there, pl.ds(column, pw)]
                pltpu.make_async_remote_copy(
                    src_ref=landed,
                    dst_ref=landed,
                    send_sem=send_sem.at[0, 0],
                    recv_sem=recv_sem.at[d, u],
                    device_id=(source, u),
                    device_id_type=MESH,
                ).wait_recv()
    ready_ref[...] = jnp.zeros_like(ready_ref)


def serve(merged, n, m, g, units, width, collective_id):
    parts = max(1, merged.shape[-1] * m // width)
    return pl.pallas_call(
        functools.partial(serve_kernel, n, m, g, units),
        out_shape=[
            jax.ShapeDtypeStruct((1, m * units, width // m), merged.dtype),
            jax.ShapeDtypeStruct((8, 128), jnp.int32),
        ],
        in_specs=[pl.BlockSpec(memory_space=pl.ANY)],
        out_specs=[pl.BlockSpec(memory_space=pl.ANY), pl.BlockSpec(memory_space=pltpu.VMEM)],
        scratch_shapes=[
            pltpu.SemaphoreType.DMA,
            pltpu.SemaphoreType.DMA((n, parts)),
            pltpu.SemaphoreType.DMA((n, m)),
        ],
        compiler_params=pltpu.CompilerParams(
            collective_id=collective_id, has_side_effects=True, vmem_limit_bytes=VMEM_BYTES
        ),
        cost_estimate=pl.CostEstimate(flops=0, bytes_accessed=4 * merged.size, transcendentals=0),
        name="serve",
    )(merged)


def merge_blocks(slab, order, anchor_of, cluster_ids, weight, n, g):
    experts = slab.shape[0]
    partial = block_gram(order, anchor_of, slab)
    share = experts // g
    part = lax.axis_index("expert") % g

    def pairs(d):
        return [(e, e // g * g + (e + d) % g) for e in range(n)]

    gram = lax.dynamic_slice_in_dim(partial, part * share, share)
    for d in range(1, g):
        other = lax.dynamic_slice_in_dim(partial, (part + d) % g * share, share)
        gram = gram + lax.ppermute(other, "expert", pairs(d))
    polar = newton_schulz(gram).astype(jnp.bfloat16)
    factors = jnp.zeros((experts, BLOCK, BLOCK), jnp.bfloat16)
    factors = lax.dynamic_update_slice_in_dim(factors, polar, part * share, 0)
    for d in range(1, g):
        other = lax.ppermute(polar, "expert", pairs(d))
        factors = lax.dynamic_update_slice_in_dim(factors, other, (part + g - d) % g * share, 0)
    return merge_rows(order, cluster_ids, weight, factors, slab, n)


def on_device(w_up, cluster, counts):
    n, m = lax.axis_size("expert"), lax.axis_size("unit")
    held, units, width = w_up.shape
    cluster_ids = cluster[:, 0]
    experts = cluster_ids.shape[0]
    index = jnp.arange(experts, dtype=jnp.int32)
    labels = jnp.arange(n, dtype=jnp.int32)
    member = cluster_ids[None, :] == labels[:, None]
    score = counts * experts + (experts - 1 - index)
    best = jnp.max(jnp.where(member, score[None, :], -1), axis=1)
    leader = experts - 1 - best % experts
    anchor_of = jnp.sum(jnp.where(member, leader[:, None], 0), axis=0)
    total = jnp.sum(jnp.where(member, counts[None, :], 0), axis=1).astype(jnp.float32)
    weight = counts.astype(jnp.float32) / jnp.sum(jnp.where(member, total[:, None], 0.0), axis=0)
    before = (cluster_ids[None, :] < cluster_ids[:, None]) | (
        (cluster_ids[None, :] == cluster_ids[:, None]) & (index[None, :] < index[:, None])
    )
    place = jnp.sum(before.astype(jnp.int32), axis=1)
    order = jnp.sum(jnp.where(place[None, :] == index[:, None], index[None, :], 0), axis=1)

    half = units // 2
    g = n // (half // BLOCK)
    cw = width // g
    me = lax.axis_index("expert")
    slab, ready = deal(w_up, n, g)
    start = half + ready[0, 0]

    def piece(peer):
        return lax.dynamic_slice(
            w_up, (0, start + peer // g * BLOCK, peer % g * cw), (held, BLOCK, cw)
        )

    coming = []
    for d in sorted(range(1, n), key=lambda d: abs(2 * d - n)):
        moved = lax.ppermute(piece((me + d) % n), "expert", [(e, (e + d) % n) for e in range(n)])
        coming.append(((me + n - d) % n, moved))
    coming.append((me, piece(me)))

    first = merge_blocks(slab.reshape(experts, BLOCK, cw), order, anchor_of, cluster_ids, weight, n, g)
    first, ready = serve(first, n, m, g, half, width, 1)

    slab = jnp.zeros((n, held, BLOCK, cw), w_up.dtype)
    for source, moved in coming:
        slab = lax.dynamic_update_slice(slab, moved[None], (source + ready[0, 0], 0, 0, 0))
    second = merge_blocks(slab.reshape(experts, BLOCK, cw), order, anchor_of, cluster_ids, weight, n, g)
    second, _ = serve(second, n, m, g, half, width, 2)
    outs = [part.reshape(m, half, width // m) for part in (first, second)]
    return jnp.concatenate(outs, axis=1).reshape(1, m * units, width // m)


def solution(mesh):
    return jax.shard_map(
        on_device,
        mesh=mesh,
        in_specs=(P("expert", "unit", None), P(), P()),
        out_specs=P("expert", None, "unit"),
        check_vma=False,
    )
```

```python
import functools

import jax
import jax.numpy as jnp
from jax import lax
from jax.experimental import pallas as pl
from jax.experimental.pallas import tpu as pltpu
from jax.sharding import PartitionSpec as P

BLOCK = 96
NS_STEPS = 8
MESH = pl.DeviceIdType.MESH
VMEM_BYTES = 48 * 1024 * 1024


def newton_schulz(matrices):
    frob_norm = jnp.sqrt(jnp.sum(matrices * matrices, axis=(-2, -1), keepdims=True) + 1e-06)
    value = matrices / frob_norm
    for iteration in range(NS_STEPS):
        square = jnp.einsum("...ij,...kj->...ik", value, value, precision=lax.Precision.HIGH)
        value = 1.5 * value - 0.5 * jnp.einsum(
            "...ik,...kj->...ij", square, value, precision=lax.Precision.HIGH
        )
    return value


def deal_kernel(n, g, w_ref, slab_ref, local_sem, send_sem, recv_sem):
    me, unit = lax.axis_index("expert"), lax.axis_index("unit")
    cw = slab_ref.shape[-1]
    barrier = pltpu.get_barrier_semaphore()
    for d in range(1, n):
        pl.semaphore_signal(barrier, inc=1, device_id=(lax.rem(me + d, n), unit), device_id_type=MESH)
    pl.semaphore_wait(barrier, n - 1)

    def piece(peer):
        rows = pl.ds(pl.multiple_of((peer // g) * BLOCK, BLOCK), BLOCK)
        columns = pl.ds(pl.multiple_of(lax.rem(peer, g) * cw, cw), cw)
        return w_ref.at[:, rows, columns]

    copies = []
    for d in sorted(range(1, n), key=lambda d: abs(2 * d - n)):
        peer = lax.rem(me + d, n)
        copy = pltpu.make_async_remote_copy(
            src_ref=piece(peer),
            dst_ref=slab_ref.at[me],
            send_sem=send_sem.at[d],
            recv_sem=recv_sem.at[d],
            device_id=(peer, unit),
            device_id_type=MESH,
        )
        copy.start()
        copies.append(copy)
    own = pltpu.make_async_copy(piece(me), slab_ref.at[me], local_sem)
    own.start()
    own.wait()
    for copy in copies:
        copy.wait()


def deal(w, n, g):
    held, units, width = w.shape
    return pl.pallas_call(
        functools.partial(deal_kernel, n, g),
        out_shape=jax.ShapeDtypeStruct((n, held, BLOCK, width // g), w.dtype),
        in_specs=[pl.BlockSpec(memory_space=pl.ANY)],
        out_specs=pl.BlockSpec(memory_space=pl.ANY),
        scratch_shapes=[
            pltpu.SemaphoreType.DMA,
            pltpu.SemaphoreType.DMA((n,)),
            pltpu.SemaphoreType.DMA((n,)),
        ],
        compiler_params=pltpu.CompilerParams(
            collective_id=0, has_side_effects=True, vmem_limit_bytes=VMEM_BYTES
        ),
        cost_estimate=pl.CostEstimate(flops=0, bytes_accessed=4 * w.size, transcendentals=0),
        name="deal",
    )(w)


def gram_kernel(order_ref, anchor_ref, slab_ref, gram_ref):
    def one(place, carry):
        expert = order_ref[place]
        gram_ref[place] = lax.dot_general(
            slab_ref[anchor_ref[expert]],
            slab_ref[expert],
            (((1,), (1,)), ((), ())),
            preferred_element_type=jnp.float32,
        )
        return carry

    lax.fori_loop(0, gram_ref.shape[0], one, 0, unroll=4)


def block_gram(order, anchor_of, slab):
    places = order.shape[0]
    _, _, cw = slab.shape
    scalars = pl.BlockSpec(memory_space=pltpu.SMEM)
    return pl.pallas_call(
        gram_kernel,
        in_specs=[scalars, scalars, pl.BlockSpec(memory_space=pltpu.VMEM)],
        out_specs=pl.BlockSpec(memory_space=pltpu.VMEM),
        out_shape=jax.ShapeDtypeStruct((places, BLOCK, BLOCK), jnp.float32),
        compiler_params=pltpu.CompilerParams(vmem_limit_bytes=VMEM_BYTES),
        cost_estimate=pl.CostEstimate(
            flops=2 * places * BLOCK * BLOCK * cw, bytes_accessed=2 * slab.size, transcendentals=0
        ),
        name="gram",
    )(order, anchor_of, slab)


def merge_kernel(order_ref, cluster_ref, weight_ref, factor_ref, slab_ref, merged_ref, total_ref):
    def one(place, last):
        expert = order_ref[place]
        here = cluster_ref[expert]
        turned = jnp.dot(factor_ref[place], slab_ref[expert], preferred_element_type=jnp.float32)
        aligned = (turned * weight_ref[expert]).astype(jnp.bfloat16).astype(jnp.float32)
        total = jnp.where(here == last, total_ref[...], 0.0) + aligned
        total_ref[...] = total
        merged_ref[here] = total.astype(merged_ref.dtype)
        return here

    total_ref[...] = jnp.zeros_like(total_ref)
    lax.fori_loop(0, factor_ref.shape[0], one, jnp.int32(-1), unroll=2)


def merge_rows(order, cluster_ids, weight, factors, slab, clusters):
    experts, _, cw = slab.shape
    scalars = pl.BlockSpec(memory_space=pltpu.SMEM)
    whole = pl.BlockSpec(memory_space=pltpu.VMEM)
    return pl.pallas_call(
        merge_kernel,
        in_specs=[scalars, scalars, scalars, whole, whole],
        out_specs=whole,
        scratch_shapes=[pltpu.VMEM((BLOCK, cw), jnp.float32)],
        out_shape=jax.ShapeDtypeStruct((clusters, BLOCK, cw), slab.dtype),
        compiler_params=pltpu.CompilerParams(vmem_limit_bytes=VMEM_BYTES),
        cost_estimate=pl.CostEstimate(
            flops=2 * slab.size * BLOCK, bytes_accessed=3 * slab.size, transcendentals=0
        ),
        name="merge",
    )(order, cluster_ids, weight, factors, slab)


def serve_kernel(n, m, g, units, merged_ref, out_ref, local_sem, send_sem, recv_sem):
    me, unit = lax.axis_index("expert"), lax.axis_index("unit")
    cw, uw = merged_ref.shape[-1], out_ref.shape[-1]
    pw = min(cw, uw)
    parts = cw // pw

    def target(part):
        column = lax.rem(me, g) * cw + part * pw
        return column // uw, pl.multiple_of(lax.rem(column, uw), pw)

    def feeds(source):
        column = lax.rem(source, g) * cw
        return (column // uw <= unit) & (unit <= (column + cw - pw) // uw)

    barrier = pltpu.get_barrier_semaphore()
    for d in range(n):
        source = lax.rem(me + n - d, n)
        for u in range(m):
            @pl.when(feeds(source) & ((u != unit) | (d != 0)))
            def _():
                pl.semaphore_signal(barrier, inc=1, device_id=(source, u), device_id_type=MESH)
    own = feeds(me)
    pl.semaphore_wait(barrier, n * parts - own.astype(jnp.int32))

    rows = pl.ds(pl.multiple_of(unit * units + (me // g) * BLOCK, BLOCK), BLOCK)

    def remote(d, part):
        peer = lax.rem(me + d, n)
        to, offset = target(part)
        return pltpu.make_async_remote_copy(
            src_ref=merged_ref.at[peer, :, pl.ds(part * pw, pw)],
            dst_ref=out_ref.at[0, rows, pl.ds(offset, pw)],
            send_sem=send_sem.at[d, part],
            recv_sem=recv_sem.at[d, unit],
            device_id=(peer, to),
            device_id_type=MESH,
        )

    def local(part):
        _, offset = target(part)
        return pltpu.make_async_copy(
            merged_ref.at[me, :, pl.ds(part * pw, pw)], out_ref.at[0, rows, pl.ds(offset, pw)], local_sem
        )

    for d in sorted(range(n), key=lambda d: abs(2 * d - n)):
        for part in range(parts):
            if d:
                remote(d, part).start()
            else:
                mine = target(part)[0] == unit

                @pl.when(mine)
                def _():
                    local(part).start()

                @pl.when(jnp.logical_not(mine))
                def _():
                    remote(0, part).start()

    for d in range(n):
        for part in range(parts):
            if d:
                remote(d, part).wait_send()
            else:
                mine = target(part)[0] == unit

                @pl.when(mine)
                def _():
                    local(part).wait()

                @pl.when(jnp.logical_not(mine))
                def _():
                    remote(0, part).wait_send()

    for d in range(n):
        source = lax.rem(me + n - d, n)
        for u in range(m):
            @pl.when(feeds(source) & ((u != unit) | (d != 0)))
            def _():
                there = pl.ds(pl.multiple_of(u * units + (source // g) * BLOCK, BLOCK), BLOCK)
                column = pl.multiple_of(lax.rem(lax.rem(source, g) * cw, uw), pw)
                landed = out_ref.at[0, there, pl.ds(column, pw)]
                pltpu.make_async_remote_copy(
                    src_ref=landed,
                    dst_ref=landed,
                    send_sem=send_sem.at[0, 0],
                    recv_sem=recv_sem.at[d, u],
                    device_id=(source, u),
                    device_id_type=MESH,
                ).wait_recv()


def serve(merged, n, m, g, units, width):
    parts = max(1, merged.shape[-1] * m // width)
    return pl.pallas_call(
        functools.partial(serve_kernel, n, m, g, units),
        out_shape=jax.ShapeDtypeStruct((1, m * units, width // m), merged.dtype),
        in_specs=[pl.BlockSpec(memory_space=pl.ANY)],
        out_specs=pl.BlockSpec(memory_space=pl.ANY),
        scratch_shapes=[
            pltpu.SemaphoreType.DMA,
            pltpu.SemaphoreType.DMA((n, parts)),
            pltpu.SemaphoreType.DMA((n, m)),
        ],
        compiler_params=pltpu.CompilerParams(
            collective_id=1, has_side_effects=True, vmem_limit_bytes=VMEM_BYTES
        ),
        cost_estimate=pl.CostEstimate(flops=0, bytes_accessed=4 * merged.size, transcendentals=0),
        name="serve",
    )(merged)


def on_device(w_up, cluster, counts):
    n, m = lax.axis_size("expert"), lax.axis_size("unit")
    held, units, width = w_up.shape
    nblocks = units // BLOCK
    g = n // nblocks
    cluster_ids = cluster[:, 0]
    experts = cluster_ids.shape[0]
    index = jnp.arange(experts, dtype=jnp.int32)
    labels = jnp.arange(n, dtype=jnp.int32)
    member = cluster_ids[None, :] == labels[:, None]
    score = counts * experts + (experts - 1 - index)
    best = jnp.max(jnp.where(member, score[None, :], -1), axis=1)
    leader = experts - 1 - best % experts
    anchor_of = jnp.sum(jnp.where(member, leader[:, None], 0), axis=0)
    total = jnp.sum(jnp.where(member, counts[None, :], 0), axis=1).astype(jnp.float32)
    weight = counts.astype(jnp.float32) / jnp.sum(jnp.where(member, total[:, None], 0.0), axis=0)

    slab = deal(w_up, n, g).reshape(experts, BLOCK, width // g)
    before = (cluster_ids[None, :] < cluster_ids[:, None]) | (
        (cluster_ids[None, :] == cluster_ids[:, None]) & (index[None, :] < index[:, None])
    )
    place = jnp.sum(before.astype(jnp.int32), axis=1)
    order = jnp.sum(jnp.where(place[None, :] == index[:, None], index[None, :], 0), axis=1)

    share = experts // g
    part = lax.axis_index("expert") % g

    def pairs(d):
        return [(e, e // g * g + (e + d) % g) for e in range(n)]

    def share_gram(d):
        return block_gram(lax.dynamic_slice_in_dim(order, (part + d) % g * share, share), anchor_of, slab)

    arriving = [lax.ppermute(share_gram(d), "expert", pairs(d)) for d in range(1, g)]
    gram = share_gram(0)
    for other in arriving:
        gram = gram + other
    polar = newton_schulz(gram).astype(jnp.bfloat16)
    factors = jnp.zeros((experts, BLOCK, BLOCK), jnp.bfloat16)
    factors = lax.dynamic_update_slice_in_dim(factors, polar, part * share, 0)
    for d in range(1, g):
        other = lax.ppermute(polar, "expert", pairs(d))
        factors = lax.dynamic_update_slice_in_dim(factors, other, (part + g - d) % g * share, 0)

    merged = merge_rows(order, cluster_ids, weight, factors, slab, n)
    return serve(merged, n, m, g, units, width)


def solution(mesh):
    return jax.shard_map(
        on_device,
        mesh=mesh,
        in_specs=(P("expert", "unit", None), P(), P()),
        out_specs=P("expert", None, "unit"),
        check_vma=False,
    )
```

```python
import functools

import jax
import jax.numpy as jnp
from jax import lax
from jax.experimental import pallas as pl
from jax.experimental.pallas import tpu as pltpu
from jax.sharding import PartitionSpec as P

BLOCK = 96
NS_STEPS = 8
PAIR = 2
MESH = pl.DeviceIdType.MESH
VMEM_BYTES = 48 * 1024 * 1024


def newton_schulz(matrices):
    frob_norm = jnp.sqrt(jnp.sum(matrices * matrices, axis=(-2, -1), keepdims=True) + 1e-06)
    value = matrices / frob_norm
    for iteration in range(NS_STEPS):
        square = jnp.einsum("...ij,...kj->...ik", value, value, precision=lax.Precision.HIGH)
        value = 1.5 * value - 0.5 * jnp.einsum(
            "...ik,...kj->...ij", square, value, precision=lax.Precision.HIGH
        )
    return value


def deal_kernel(n, gp, w_ref, slab_ref, local_sem, send_sem, recv_sem):
    me, unit = lax.axis_index("expert"), lax.axis_index("unit")
    cw = slab_ref.shape[-1]
    half = n // PAIR
    side = lax.rem(unit, PAIR)
    feeder = unit - side + me // half
    own = me // half == side
    barrier = pltpu.get_barrier_semaphore()
    for d in range(n):
        source = lax.rem(me + d, n)

        @pl.when((d != 0) | jnp.logical_not(own))
        def _():
            pl.semaphore_signal(barrier, inc=1, device_id=(source, feeder), device_id_type=MESH)
    pl.semaphore_wait(barrier, n - own.astype(jnp.int32))

    def piece(place, to):
        rows = pl.ds(pl.multiple_of(place // gp * BLOCK, BLOCK), BLOCK)
        columns = pl.ds(pl.multiple_of((lax.rem(place, gp) * PAIR + to) * cw, cw), cw)
        return w_ref.at[:, rows, columns]

    def remote(i, to):
        place = lax.rem(me + i, half)
        return pltpu.make_async_remote_copy(
            src_ref=piece(place, to),
            dst_ref=slab_ref.at[me],
            send_sem=send_sem.at[i, to],
            recv_sem=recv_sem.at[me],
            device_id=(side * half + place, unit - side + to),
            device_id_type=MESH,
        )

    def local():
        return pltpu.make_async_copy(piece(lax.rem(me, half), side), slab_ref.at[me], local_sem)

    for i in sorted(range(half), key=lambda i: abs(2 * i - half)):
        for to in range(PAIR):
            @pl.when((i != 0) | (to != side) | jnp.logical_not(own))
            def _():
                remote(i, to).start()

    @pl.when(own)
    def _():
        local().start()
        local().wait()

    for i in range(half):
        for to in range(PAIR):
            @pl.when((i != 0) | (to != side) | jnp.logical_not(own))
            def _():
                remote(i, to).wait_send()

    for d in range(n):
        source = lax.rem(me + d, n)

        @pl.when((d != 0) | jnp.logical_not(own))
        def _():
            landed = slab_ref.at[source]
            pltpu.make_async_remote_copy(
                src_ref=landed,
                dst_ref=landed,
                send_sem=send_sem.at[0, 0],
                recv_sem=recv_sem.at[source],
                device_id=(source, feeder),
                device_id_type=MESH,
            ).wait_recv()


def deal(w, n, g, gp):
    held, units, width = w.shape
    return pl.pallas_call(
        functools.partial(deal_kernel, n, gp),
        out_shape=jax.ShapeDtypeStruct((n, held, BLOCK, width // g), w.dtype),
        in_specs=[pl.BlockSpec(memory_space=pl.ANY)],
        out_specs=pl.BlockSpec(memory_space=pl.ANY),
        scratch_shapes=[
            pltpu.SemaphoreType.DMA,
            pltpu.SemaphoreType.DMA((n // PAIR, PAIR)),
            pltpu.SemaphoreType.DMA((n,)),
        ],
        compiler_params=pltpu.CompilerParams(
            collective_id=0, has_side_effects=True, vmem_limit_bytes=VMEM_BYTES
        ),
        cost_estimate=pl.CostEstimate(flops=0, bytes_accessed=4 * w.size, transcendentals=0),
        name="deal",
    )(w)


def gram_kernel(order_ref, anchor_ref, slab_ref, gram_ref):
    def one(place, carry):
        expert = order_ref[place]
        gram_ref[place] = lax.dot_general(
            slab_ref[anchor_ref[expert]],
            slab_ref[expert],
            (((1,), (1,)), ((), ())),
            preferred_element_type=jnp.float32,
        )
        return carry

    lax.fori_loop(0, gram_ref.shape[0], one, 0, unroll=4)


def block_gram(order, anchor_of, slab):
    places = order.shape[0]
    _, _, cw = slab.shape
    scalars = pl.BlockSpec(memory_space=pltpu.SMEM)
    return pl.pallas_call(
        gram_kernel,
        in_specs=[scalars, scalars, pl.BlockSpec(memory_space=pltpu.VMEM)],
        out_specs=pl.BlockSpec(memory_space=pltpu.VMEM),
        out_shape=jax.ShapeDtypeStruct((places, BLOCK, BLOCK), jnp.float32),
        compiler_params=pltpu.CompilerParams(vmem_limit_bytes=VMEM_BYTES),
        cost_estimate=pl.CostEstimate(
            flops=2 * places * BLOCK * BLOCK * cw, bytes_accessed=2 * slab.size, transcendentals=0
        ),
        name="gram",
    )(order, anchor_of, slab)


def merge_kernel(order_ref, cluster_ref, weight_ref, factor_ref, slab_ref, merged_ref, total_ref):
    def one(place, last):
        expert = order_ref[place]
        here = cluster_ref[expert]
        turned = jnp.dot(factor_ref[place], slab_ref[expert], preferred_element_type=jnp.float32)
        aligned = (turned * weight_ref[expert]).astype(jnp.bfloat16).astype(jnp.float32)
        total = jnp.where(here == last, total_ref[...], 0.0) + aligned
        total_ref[...] = total
        merged_ref[here] = total.astype(merged_ref.dtype)
        return here

    total_ref[...] = jnp.zeros_like(total_ref)
    lax.fori_loop(0, factor_ref.shape[0], one, jnp.int32(-1), unroll=2)


def merge_rows(order, cluster_ids, weight, factors, slab, clusters):
    experts, _, cw = slab.shape
    scalars = pl.BlockSpec(memory_space=pltpu.SMEM)
    whole = pl.BlockSpec(memory_space=pltpu.VMEM)
    return pl.pallas_call(
        merge_kernel,
        in_specs=[scalars, scalars, scalars, whole, whole],
        out_specs=whole,
        scratch_shapes=[pltpu.VMEM((BLOCK, cw), jnp.float32)],
        out_shape=jax.ShapeDtypeStruct((clusters, BLOCK, cw), slab.dtype),
        compiler_params=pltpu.CompilerParams(vmem_limit_bytes=VMEM_BYTES),
        cost_estimate=pl.CostEstimate(
            flops=2 * slab.size * BLOCK, bytes_accessed=3 * slab.size, transcendentals=0
        ),
        name="merge",
    )(order, cluster_ids, weight, factors, slab)


def serve_kernel(n, m, gp, units, merged_ref, out_ref, local_sem, send_sem, recv_sem):
    me, unit = lax.axis_index("expert"), lax.axis_index("unit")
    cw, uw = merged_ref.shape[-1], out_ref.shape[-1]
    pw = min(cw, uw)
    parts = cw // pw

    def first_column(source, u):
        return (lax.rem(source, gp) * PAIR + lax.rem(u, PAIR)) * cw

    def target(part):
        column = first_column(me, unit) + part * pw
        return column // uw, pl.multiple_of(lax.rem(column, uw), pw)

    def feeds(source, u):
        column = first_column(source, u)
        return (column // uw <= unit) & (unit <= (column + cw - pw) // uw)

    barrier = pltpu.get_barrier_semaphore()
    for d in range(n):
        source = lax.rem(me + n - d, n)
        for u in range(m):
            @pl.when(feeds(source, u) & ((u != unit) | (d != 0)))
            def _():
                pl.semaphore_signal(barrier, inc=1, device_id=(source, u), device_id_type=MESH)
    own = feeds(me, unit)
    pl.semaphore_wait(barrier, n * parts - own.astype(jnp.int32))

    rows = pl.ds(pl.multiple_of((unit - lax.rem(unit, PAIR)) * units + me // gp * BLOCK, BLOCK), BLOCK)

    def remote(d, part):
        peer = lax.rem(me + d, n)
        to, offset = target(part)
        return pltpu.make_async_remote_copy(
            src_ref=merged_ref.at[peer, :, pl.ds(part * pw, pw)],
            dst_ref=out_ref.at[0, rows, pl.ds(offset, pw)],
            send_sem=send_sem.at[d, part],
            recv_sem=recv_sem.at[d, unit],
            device_id=(peer, to),
            device_id_type=MESH,
        )

    def local(part):
        _, offset = target(part)
        return pltpu.make_async_copy(
            merged_ref.at[me, :, pl.ds(part * pw, pw)], out_ref.at[0, rows, pl.ds(offset, pw)], local_sem
        )

    for d in sorted(range(n), key=lambda d: abs(2 * d - n)):
        for part in range(parts):
            if d:
                remote(d, part).start()
            else:
                mine = target(part)[0] == unit

                @pl.when(mine)
                def _():
                    local(part).start()

                @pl.when(jnp.logical_not(mine))
                def _():
                    remote(0, part).start()

    for d in range(n):
        for part in range(parts):
            if d:
                remote(d, part).wait_send()
            else:
                mine = target(part)[0] == unit

                @pl.when(mine)
                def _():
                    local(part).wait()

                @pl.when(jnp.logical_not(mine))
                def _():
                    remote(0, part).wait_send()

    for d in range(n):
        source = lax.rem(me + n - d, n)
        for u in range(m):
            @pl.when(feeds(source, u) & ((u != unit) | (d != 0)))
            def _():
                there = pl.ds(pl.multiple_of((u - u % PAIR) * units + source // gp * BLOCK, BLOCK), BLOCK)
                column = pl.multiple_of(lax.rem(first_column(source, u), uw), pw)
                landed = out_ref.at[0, there, pl.ds(column, pw)]
                pltpu.make_async_remote_copy(
                    src_ref=landed,
                    dst_ref=landed,
                    send_sem=send_sem.at[0, 0],
                    recv_sem=recv_sem.at[d, u],
                    device_id=(source, u),
                    device_id_type=MESH,
                ).wait_recv()


def serve(merged, n, m, gp, units, width):
    parts = max(1, merged.shape[-1] * m // width)
    return pl.pallas_call(
        functools.partial(serve_kernel, n, m, gp, units),
        out_shape=jax.ShapeDtypeStruct((1, m * units, width // m), merged.dtype),
        in_specs=[pl.BlockSpec(memory_space=pl.ANY)],
        out_specs=pl.BlockSpec(memory_space=pl.ANY),
        scratch_shapes=[
            pltpu.SemaphoreType.DMA,
            pltpu.SemaphoreType.DMA((n, parts)),
            pltpu.SemaphoreType.DMA((n, m)),
        ],
        compiler_params=pltpu.CompilerParams(
            collective_id=1, has_side_effects=True, vmem_limit_bytes=VMEM_BYTES
        ),
        cost_estimate=pl.CostEstimate(flops=0, bytes_accessed=4 * merged.size, transcendentals=0),
        name="serve",
    )(merged)


def on_device(w_up, cluster, counts):
    n, m = lax.axis_size("expert"), lax.axis_size("unit")
    held, units, width = w_up.shape
    gp = n // (PAIR * units // BLOCK)
    g = gp * PAIR
    cluster_ids = cluster[:, 0]
    experts = cluster_ids.shape[0]
    index = jnp.arange(experts, dtype=jnp.int32)
    labels = jnp.arange(n, dtype=jnp.int32)
    member = cluster_ids[None, :] == labels[:, None]
    score = counts * experts + (experts - 1 - index)
    best = jnp.max(jnp.where(member, score[None, :], -1), axis=1)
    leader = experts - 1 - best % experts
    anchor_of = jnp.sum(jnp.where(member, leader[:, None], 0), axis=0)
    total = jnp.sum(jnp.where(member, counts[None, :], 0), axis=1).astype(jnp.float32)
    weight = counts.astype(jnp.float32) / jnp.sum(jnp.where(member, total[:, None], 0.0), axis=0)

    slab = deal(w_up, n, g, gp).reshape(experts, BLOCK, width // g)
    before = (cluster_ids[None, :] < cluster_ids[:, None]) | (
        (cluster_ids[None, :] == cluster_ids[:, None]) & (index[None, :] < index[:, None])
    )
    place = jnp.sum(before.astype(jnp.int32), axis=1)
    order = jnp.sum(jnp.where(place[None, :] == index[:, None], index[None, :], 0), axis=1)

    share = experts // g
    part = lax.axis_index("expert") % gp * PAIR + lax.axis_index("unit") % PAIR

    def pairs(d):
        moves = []
        for e in range(n):
            for u in range(m):
                to = (e % gp * PAIR + u % PAIR + d) % g
                moves.append((e * m + u, (e // gp * gp + to // PAIR) * m + u // PAIR * PAIR + to % PAIR))
        return moves

    def share_gram(d):
        return block_gram(lax.dynamic_slice_in_dim(order, (part + d) % g * share, share), anchor_of, slab)

    arriving = [lax.ppermute(share_gram(d), ("expert", "unit"), pairs(d)) for d in range(1, g)]
    gram = share_gram(0)
    for other in arriving:
        gram = gram + other
    polar = newton_schulz(gram).astype(jnp.bfloat16)
    factors = jnp.zeros((experts, BLOCK, BLOCK), jnp.bfloat16)
    factors = lax.dynamic_update_slice_in_dim(factors, polar, part * share, 0)
    for d in range(1, g):
        other = lax.ppermute(polar, ("expert", "unit"), pairs(d))
        factors = lax.dynamic_update_slice_in_dim(factors, other, (part + g - d) % g * share, 0)

    merged = merge_rows(order, cluster_ids, weight, factors, slab, n)
    return serve(merged, n, m, gp, units, width)


def solution(mesh):
    return jax.shard_map(
        on_device,
        mesh=mesh,
        in_specs=(P("expert", "unit", None), P(), P()),
        out_specs=P("expert", None, "unit"),
        check_vma=False,
    )
```

```python
import functools

import jax
import jax.numpy as jnp
from jax import lax
from jax.experimental import pallas as pl
from jax.experimental.pallas import tpu as pltpu
from jax.sharding import PartitionSpec as P

BLOCK = 96
NS_STEPS = 8
PAIR = 2
MESH = pl.DeviceIdType.MESH
VMEM_BYTES = 48 * 1024 * 1024


def newton_schulz(matrices):
    frob_norm = jnp.sqrt(jnp.sum(matrices * matrices, axis=(-2, -1), keepdims=True) + 1e-06)
    value = matrices / frob_norm
    for iteration in range(NS_STEPS):
        square = jnp.einsum("...ij,...kj->...ik", value, value, precision=lax.Precision.HIGH)
        value = 1.5 * value - 0.5 * jnp.einsum(
            "...ik,...kj->...ij", square, value, precision=lax.Precision.HIGH
        )
    return value


def deal_kernel(n, gp, w_ref, slab_ref, local_sem, send_sem, recv_sem):
    me, unit = lax.axis_index("expert"), lax.axis_index("unit")
    cw = slab_ref.shape[-1]
    half = n // PAIR
    side = lax.rem(unit, PAIR)
    feeder = unit - side + me // half
    own = me // half == side
    barrier = pltpu.get_barrier_semaphore()
    for d in range(n):
        source = lax.rem(me + d, n)

        @pl.when((d != 0) | jnp.logical_not(own))
        def _():
            pl.semaphore_signal(barrier, inc=1, device_id=(source, feeder), device_id_type=MESH)
    pl.semaphore_wait(barrier, n - own.astype(jnp.int32))

    def piece(place, to):
        rows = pl.ds(pl.multiple_of(place // gp * BLOCK, BLOCK), BLOCK)
        columns = pl.ds(pl.multiple_of((lax.rem(place, gp) * PAIR + to) * cw, cw), cw)
        return w_ref.at[:, rows, columns]

    def remote(i, to):
        place = lax.rem(me + i, half)
        return pltpu.make_async_remote_copy(
            src_ref=piece(place, to),
            dst_ref=slab_ref.at[me],
            send_sem=send_sem.at[i, to],
            recv_sem=recv_sem.at[me],
            device_id=(side * half + place, unit - side + to),
            device_id_type=MESH,
        )

    def local():
        return pltpu.make_async_copy(piece(lax.rem(me, half), side), slab_ref.at[me], local_sem)

    for i in sorted(range(half), key=lambda i: abs(2 * i - half)):
        for to in range(PAIR):
            @pl.when((i != 0) | (to != side) | jnp.logical_not(own))
            def _():
                remote(i, to).start()

    @pl.when(own)
    def _():
        local().start()
        local().wait()

    for i in range(half):
        for to in range(PAIR):
            @pl.when((i != 0) | (to != side) | jnp.logical_not(own))
            def _():
                remote(i, to).wait_send()

    for d in range(n):
        source = lax.rem(me + d, n)

        @pl.when((d != 0) | jnp.logical_not(own))
        def _():
            landed = slab_ref.at[source]
            pltpu.make_async_remote_copy(
                src_ref=landed,
                dst_ref=landed,
                send_sem=send_sem.at[0, 0],
                recv_sem=recv_sem.at[source],
                device_id=(source, feeder),
                device_id_type=MESH,
            ).wait_recv()


def deal(w, n, g, gp):
    held, units, width = w.shape
    return pl.pallas_call(
        functools.partial(deal_kernel, n, gp),
        out_shape=jax.ShapeDtypeStruct((n, held, BLOCK, width // g), w.dtype),
        in_specs=[pl.BlockSpec(memory_space=pl.ANY)],
        out_specs=pl.BlockSpec(memory_space=pl.ANY),
        scratch_shapes=[
            pltpu.SemaphoreType.DMA,
            pltpu.SemaphoreType.DMA((n // PAIR, PAIR)),
            pltpu.SemaphoreType.DMA((n,)),
        ],
        compiler_params=pltpu.CompilerParams(
            collective_id=0, has_side_effects=True, vmem_limit_bytes=VMEM_BYTES
        ),
        cost_estimate=pl.CostEstimate(flops=0, bytes_accessed=4 * w.size, transcendentals=0),
        name="deal",
    )(w)


def gram_kernel(order_ref, anchor_ref, slab_ref, gram_ref):
    def one(place, carry):
        expert = order_ref[place]
        gram_ref[place] = lax.dot_general(
            slab_ref[anchor_ref[expert]],
            slab_ref[expert],
            (((1,), (1,)), ((), ())),
            preferred_element_type=jnp.float32,
        )
        return carry

    lax.fori_loop(0, gram_ref.shape[0], one, 0, unroll=4)


def block_gram(order, anchor_of, slab):
    places = order.shape[0]
    _, _, cw = slab.shape
    scalars = pl.BlockSpec(memory_space=pltpu.SMEM)
    return pl.pallas_call(
        gram_kernel,
        in_specs=[scalars, scalars, pl.BlockSpec(memory_space=pltpu.VMEM)],
        out_specs=pl.BlockSpec(memory_space=pltpu.VMEM),
        out_shape=jax.ShapeDtypeStruct((places, BLOCK, BLOCK), jnp.float32),
        compiler_params=pltpu.CompilerParams(vmem_limit_bytes=VMEM_BYTES),
        cost_estimate=pl.CostEstimate(
            flops=2 * places * BLOCK * BLOCK * cw, bytes_accessed=2 * slab.size, transcendentals=0
        ),
        name="gram",
    )(order, anchor_of, slab)


def merge_kernel(order_ref, cluster_ref, weight_ref, factor_ref, slab_ref, merged_ref, total_ref):
    def one(place, last):
        expert = order_ref[place]
        here = cluster_ref[expert]
        turned = jnp.dot(factor_ref[place], slab_ref[expert], preferred_element_type=jnp.float32)
        aligned = (turned * weight_ref[expert]).astype(jnp.bfloat16).astype(jnp.float32)
        total = jnp.where(here == last, total_ref[...], 0.0) + aligned
        total_ref[...] = total
        merged_ref[here] = total.astype(merged_ref.dtype)
        return here

    total_ref[...] = jnp.zeros_like(total_ref)
    lax.fori_loop(0, factor_ref.shape[0], one, jnp.int32(-1), unroll=2)


def merge_rows(order, cluster_ids, weight, factors, slab, clusters):
    experts, _, cw = slab.shape
    scalars = pl.BlockSpec(memory_space=pltpu.SMEM)
    whole = pl.BlockSpec(memory_space=pltpu.VMEM)
    return pl.pallas_call(
        merge_kernel,
        in_specs=[scalars, scalars, scalars, whole, whole],
        out_specs=whole,
        scratch_shapes=[pltpu.VMEM((BLOCK, cw), jnp.float32)],
        out_shape=jax.ShapeDtypeStruct((clusters, BLOCK, cw), slab.dtype),
        compiler_params=pltpu.CompilerParams(vmem_limit_bytes=VMEM_BYTES),
        cost_estimate=pl.CostEstimate(
            flops=2 * slab.size * BLOCK, bytes_accessed=3 * slab.size, transcendentals=0
        ),
        name="merge",
    )(order, cluster_ids, weight, factors, slab)


def serve_kernel(n, m, gp, units, merged_ref, out_ref, local_sem, send_sem, recv_sem):
    me, unit = lax.axis_index("expert"), lax.axis_index("unit")
    cw, uw = merged_ref.shape[-1], out_ref.shape[-1]
    pw = min(cw, uw)
    parts = cw // pw

    def first_column(source, u):
        return (lax.rem(source, gp) * PAIR + lax.rem(u, PAIR)) * cw

    def target(part):
        column = first_column(me, unit) + part * pw
        return column // uw, pl.multiple_of(lax.rem(column, uw), pw)

    def feeds(source, u):
        column = first_column(source, u)
        return (column // uw <= unit) & (unit <= (column + cw - pw) // uw)

    barrier = pltpu.get_barrier_semaphore()
    for d in range(n):
        source = lax.rem(me + n - d, n)
        for u in range(m):
            @pl.when(feeds(source, u) & ((u != unit) | (d != 0)))
            def _():
                pl.semaphore_signal(barrier, inc=1, device_id=(source, u), device_id_type=MESH)
    own = feeds(me, unit)
    pl.semaphore_wait(barrier, n * parts - own.astype(jnp.int32))

    rows = pl.ds(pl.multiple_of((unit - lax.rem(unit, PAIR)) * units + me // gp * BLOCK, BLOCK), BLOCK)

    def remote(d, part):
        peer = lax.rem(me + d, n)
        to, offset = target(part)
        return pltpu.make_async_remote_copy(
            src_ref=merged_ref.at[peer, :, pl.ds(part * pw, pw)],
            dst_ref=out_ref.at[0, rows, pl.ds(offset, pw)],
            send_sem=send_sem.at[d, part],
            recv_sem=recv_sem.at[d, unit],
            device_id=(peer, to),
            device_id_type=MESH,
        )

    def local(part):
        _, offset = target(part)
        return pltpu.make_async_copy(
            merged_ref.at[me, :, pl.ds(part * pw, pw)], out_ref.at[0, rows, pl.ds(offset, pw)], local_sem
        )

    for d in sorted(range(n), key=lambda d: abs(2 * d - n)):
        for part in range(parts):
            if d:
                remote(d, part).start()
            else:
                mine = target(part)[0] == unit

                @pl.when(mine)
                def _():
                    local(part).start()

                @pl.when(jnp.logical_not(mine))
                def _():
                    remote(0, part).start()

    for d in range(n):
        for part in range(parts):
            if d:
                remote(d, part).wait_send()
            else:
                mine = target(part)[0] == unit

                @pl.when(mine)
                def _():
                    local(part).wait()

                @pl.when(jnp.logical_not(mine))
                def _():
                    remote(0, part).wait_send()

    for d in range(n):
        source = lax.rem(me + n - d, n)
        for u in range(m):
            @pl.when(feeds(source, u) & ((u != unit) | (d != 0)))
            def _():
                there = pl.ds(pl.multiple_of((u - u % PAIR) * units + source // gp * BLOCK, BLOCK), BLOCK)
                column = pl.multiple_of(lax.rem(first_column(source, u), uw), pw)
                landed = out_ref.at[0, there, pl.ds(column, pw)]
                pltpu.make_async_remote_copy(
                    src_ref=landed,
                    dst_ref=landed,
                    send_sem=send_sem.at[0, 0],
                    recv_sem=recv_sem.at[d, u],
                    device_id=(source, u),
                    device_id_type=MESH,
                ).wait_recv()


def serve(merged, n, m, gp, units, width):
    parts = max(1, merged.shape[-1] * m // width)
    return pl.pallas_call(
        functools.partial(serve_kernel, n, m, gp, units),
        out_shape=jax.ShapeDtypeStruct((1, m * units, width // m), merged.dtype),
        in_specs=[pl.BlockSpec(memory_space=pltpu.VMEM)],
        out_specs=pl.BlockSpec(memory_space=pl.ANY),
        scratch_shapes=[
            pltpu.SemaphoreType.DMA,
            pltpu.SemaphoreType.DMA((n, parts)),
            pltpu.SemaphoreType.DMA((n, m)),
        ],
        compiler_params=pltpu.CompilerParams(
            collective_id=1, has_side_effects=True, vmem_limit_bytes=VMEM_BYTES
        ),
        cost_estimate=pl.CostEstimate(flops=0, bytes_accessed=4 * merged.size, transcendentals=0),
        name="serve",
    )(merged)


def on_device(w_up, cluster, counts):
    n, m = lax.axis_size("expert"), lax.axis_size("unit")
    held, units, width = w_up.shape
    gp = n // (PAIR * units // BLOCK)
    g = gp * PAIR
    cluster_ids = cluster[:, 0]
    experts = cluster_ids.shape[0]
    index = jnp.arange(experts, dtype=jnp.int32)
    labels = jnp.arange(n, dtype=jnp.int32)
    member = cluster_ids[None, :] == labels[:, None]
    score = counts * experts + (experts - 1 - index)
    best = jnp.max(jnp.where(member, score[None, :], -1), axis=1)
    leader = experts - 1 - best % experts
    anchor_of = jnp.sum(jnp.where(member, leader[:, None], 0), axis=0)
    total = jnp.sum(jnp.where(member, counts[None, :], 0), axis=1).astype(jnp.float32)
    weight = counts.astype(jnp.float32) / jnp.sum(jnp.where(member, total[:, None], 0.0), axis=0)

    slab = deal(w_up, n, g, gp).reshape(experts, BLOCK, width // g)
    before = (cluster_ids[None, :] < cluster_ids[:, None]) | (
        (cluster_ids[None, :] == cluster_ids[:, None]) & (index[None, :] < index[:, None])
    )
    place = jnp.sum(before.astype(jnp.int32), axis=1)
    order = jnp.sum(jnp.where(place[None, :] == index[:, None], index[None, :], 0), axis=1)

    share = experts // g
    part = lax.axis_index("expert") % gp * PAIR + lax.axis_index("unit") % PAIR

    def pairs(d):
        moves = []
        for e in range(n):
            for u in range(m):
                to = (e % gp * PAIR + u % PAIR + d) % g
                moves.append((e * m + u, (e // gp * gp + to // PAIR) * m + u // PAIR * PAIR + to % PAIR))
        return moves

    def share_gram(d):
        return block_gram(lax.dynamic_slice_in_dim(order, (part + d) % g * share, share), anchor_of, slab)

    arriving = [lax.ppermute(share_gram(d), ("expert", "unit"), pairs(d)) for d in range(1, g)]
    gram = share_gram(0)
    for other in arriving:
        gram = gram + other
    polar = newton_schulz(gram).astype(jnp.bfloat16)
    factors = jnp.zeros((experts, BLOCK, BLOCK), jnp.bfloat16)
    factors = lax.dynamic_update_slice_in_dim(factors, polar, part * share, 0)
    for d in range(1, g):
        other = lax.ppermute(polar, ("expert", "unit"), pairs(d))
        factors = lax.dynamic_update_slice_in_dim(factors, other, (part + g - d) % g * share, 0)

    merged = merge_rows(order, cluster_ids, weight, factors, slab, n)
    return serve(merged, n, m, gp, units, width)


def solution(mesh):
    return jax.shard_map(
        on_device,
        mesh=mesh,
        in_specs=(P("expert", "unit", None), P(), P()),
        out_specs=P("expert", None, "unit"),
        check_vma=False,
    )
```
